128 devices in a mesh: dp: 16 (over z, y_hi, core), mp: 8 (over x, y_lo).
Axes of the slice: x: 4, y: 4 (y_hi: 2, y_lo: 2; y = y_hi * 2 + y_lo), z: 4, core: 2. Of those that a mesh axis runs over, the one named last changes fastest.
Arguments:
- layer_inputs: bfloat16 [20480, 5120], P('dp', 'mp'), may hold values from -6 to 6
- cotangent: bfloat16 [20480, 7168], P('dp', 'mp'), may hold values from -0.41796875 to 0.41796875
- master: float32 [5120, 7168], P('dp', 'mp'), may hold values from -0.078125 to 0.078125
- moment_one: float32 [5120, 7168], P('dp', 'mp'), may hold values from -1.8 to 1.8
- moment_two: float32 [5120, 7168], P('dp', 'mp'), may hold values from 10 to 1000
- embedding_table: bfloat16 [76032, 5120], P('dp', 'mp'), may hold values from -6 to 6
- token_ids: int32 [256, 4], replicated, may hold values from 0 to 76031
- lengths: int32 [256], P('dp'), may hold values from 2 to 1024, as said below
- key_cache: bfloat16 [256, 8, 1024, 128], P('dp', 'mp'), may hold values from -2048 to 2048
- value_cache: bfloat16 [256, 8, 1024, 128], P('dp', 'mp'), may hold values from -6 to 6
Outputs:
- new_master: float32 [5120, 7168], P('dp', 'mp')
- new_moment_one: float32 [5120, 7168], P('dp', 'mp')
- new_moment_two: float32 [5120, 7168], P('dp', 'mp')
- attended: float32 [256, 4, 5120], P('dp', None, 'mp')
The draws below stay inside these ranges and needn't reach their ends.
Inputs may be any that keep to these rules, and one draw needn't show every extreme that they name: lengths[s] slots of sequence s are filled; some sequence has all 1024.
All inputs are finite; a program needn't handle non-finite values.
Results may differ from the reference program's by a relative error of at most 0.022.
Values may be sent and summed in bfloat16 or wider, within the bound.
A program may use at most 128 MiB of HBM per device.

```python
import math
import jax
import jax.numpy as jnp
import numpy as np
from jax import lax

D = 5120
QH = 40
KVH = 8
HD = 128
VOCAB = 76032
STEPS = 4
TOK_DEV = 1280
SEQ_GRP = 16
CACHE = 1024
QKV = 7168
TOKENS = 20480
SEQS = 256
N_DP = 16


def draw_lengths(key, part):
    key = jax.random.fold_in(key, 11)
    group_key, seq_key = jax.random.split(key)
    group_count = SEQS // SEQ_GRP
    ceiling = jax.random.randint(group_key, (group_count, 1), max(2, CACHE // 8), CACHE + 1)
    drawn = jax.random.randint(seq_key, (group_count, SEQ_GRP), 2, ceiling + 1).reshape(SEQS)
    leading = jnp.arange(SEQS) == 0
    return jnp.where(leading, CACHE, drawn).astype(jnp.int32)


def draw_key_cache(key, part):
    key = jax.random.fold_in(key, 23)
    base_keys = jnp.clip(jax.random.normal(key, (SEQS, KVH, CACHE, HD), jnp.float32), -6.0, 6.0)
    return base_keys.astype(jnp.bfloat16)


def touch_ends(values, stream_key, smallest, top_value):
    shape = values.shape
    spot = [jax.random.randint(jax.random.fold_in(stream_key, axis), (), 0, shape[axis]) for axis in range(len(shape))]
    values = values.at[tuple(spot)].set(smallest)
    longest = shape.index(max(shape))
    spot[longest] = (spot[longest] + 1) % shape[longest]
    return values.at[tuple(spot)].set(top_value)


def shard_levels(own_key, extent, shards, least, high):
    gain, own = 1.0, jax.random.fold_in(own_key, 6)
    for dim, blocks in shards:
        steps = jnp.exp(jax.random.uniform(jax.random.fold_in(own, dim), (blocks,), jnp.float32, least / len(shards), high / len(shards)))
        gain = gain * jnp.repeat(steps, extent[dim] // blocks).reshape([-1 if axis == dim else 1 for axis in range(len(extent))])
    return gain


def wide_ids(own_key, shape, count, slope):
    weights = [min(1 << octave, count + 1 - (1 << octave)) * (1 << 20) // math.isqrt((1 << octave) ** slope) + 1 for octave in range((count + 1).bit_length()) if 1 << octave <= count]
    deviation = 1 + sum(weights) // (1 << 30)
    grid = np.cumsum(np.array([max(1, weight // deviation) for weight in weights]))
    ticket = jax.random.randint(jax.random.fold_in(own_key, 1), shape, 0, int(grid[len(weights) - 1]))
    start = jnp.left_shift(1, jnp.searchsorted(jnp.asarray(grid, jnp.int32), ticket, side="right").astype(jnp.int32))
    grade = start - 1 + jax.random.randint(jax.random.fold_in(own_key, 4), shape, 0, 1 << 30) % jnp.minimum(start, count + 1 - start)
    return jax.random.permutation(jax.random.fold_in(own_key, 2), count)[grade].astype(jnp.int32)


def scatter_about(rng, shape, spread, reach, cuts=(), kind=jnp.bfloat16):
    loudness = shard_levels(rng, shape, cuts, -0.22, 0.18) if cuts else 1.0
    result = jax.random.normal(rng, shape, jnp.float32) * spread * loudness
    return jnp.minimum(jnp.maximum(result, -reach), reach).astype(kind)


def setup_inputs(seed: int = 0) -> dict:
    keys = jax.random.split(jax.random.key(seed), 11)
    layer_inputs = scatter_about(keys[0], (TOKENS, D), 1.0, 6.0, ((0, 16), (1, 8)))
    cotangent = scatter_about(keys[1], (TOKENS, QKV), (10.0 * TOKENS ** -0.5), 0.41796875, ((0, 16), (1, 8)))
    master = scatter_about(keys[2], (D, QKV), D ** -0.5, 0.078125, ((0, 16), (1, 8)), jnp.float32)
    moment_one = scatter_about(keys[3], (D, QKV), 0.3, 1.8, ((0, 16), (1, 8)), jnp.float32)
    moment_two = jnp.clip(jnp.exp(math.log(1000.0) - 4.6051702 * jax.random.uniform(keys[4], (D, QKV), jnp.float32) ** shard_levels(keys[4], (D, QKV), ((0, 16), (1, 8)), -0.2, 0.2)), 10.0, 1000.0)
    embedding_table = scatter_about(keys[5], (VOCAB, D), 1.0, 6.0, ((0, 16), (1, 8)))
    token_ids = touch_ends(wide_ids(keys[6], (SEQS, STEPS), VOCAB, 2), jax.random.fold_in(keys[6], 3), 0, VOCAB - 1).astype(jnp.int32)
    lengths = draw_lengths(jax.random.fold_in(keys[10], 71), 0)
    key_cache = draw_key_cache(jax.random.fold_in(keys[10], 71), 0)
    value_cache = scatter_about(keys[9], (SEQS, KVH, CACHE, HD), 1.0, 6.0, ((0, 16), (1, 8)))
    return dict(layer_inputs=layer_inputs, cotangent=cotangent, master=master, moment_one=moment_one, moment_two=moment_two, embedding_table=embedding_table, token_ids=token_ids, lengths=lengths, key_cache=key_cache, value_cache=value_cache)


beta_one = 0.9
beta_two = 0.95
adam_eps = 1e-08
learn_rate = 0.001
decay_rate = 0.1
adam_step = 8
norm_eps = 1e-06
rope_base = 1000000.0

def rotate(vectors, positions):
    half_width = vectors.shape[-1] // 2
    frequency = jnp.exp(jnp.arange(half_width, dtype=jnp.float32) * (-2.0 * math.log(rope_base) / vectors.shape[-1]))
    angles = positions[:, :, None, None, None].astype(jnp.float32) * frequency
    cosine_table = jnp.cos(angles)
    sine_table = jnp.sin(angles)
    front_half = vectors[..., :half_width]
    back_half = vectors[..., half_width:]
    return jnp.concatenate([front_half * cosine_table - back_half * sine_table, back_half * cosine_table + front_half * sine_table], axis=-1)

def attend(joined, lengths, key_cache, value_cache, group_size):
    seq_count = joined.shape[0]
    step_count = joined.shape[1]
    kv_heads = key_cache.shape[1]
    cache_span = key_cache.shape[2]
    head_width = key_cache.shape[3]
    shaped = joined.reshape(seq_count, step_count, kv_heads, group_size + 2, head_width)
    positions = lengths[:, None] + jnp.arange(step_count, dtype=jnp.int32)[None, :]
    queries = rotate(shaped[:, :, :, :group_size], positions)
    new_keys = rotate(shaped[:, :, :, group_size:group_size + 1], positions)[:, :, :, 0].astype(jnp.bfloat16)
    new_values = shaped[:, :, :, group_size + 1].astype(jnp.bfloat16)
    score_scale = 1.0 / math.sqrt(head_width)
    old_scores = jnp.einsum('bskgd,bkcd->bskgc', queries.astype(jnp.float32), key_cache.astype(jnp.float32)) * score_scale
    new_scores = jnp.einsum('bskgd,btkd->bskgt', queries.astype(jnp.float32), new_keys.astype(jnp.float32)) * score_scale
    cache_live = jnp.arange(cache_span, dtype=jnp.int32)[None, :] < lengths[:, None]
    old_scores = jnp.where(cache_live[:, None, None, None, :], old_scores, -jnp.inf)
    causal = jnp.arange(step_count)[None, :] <= jnp.arange(step_count)[:, None]
    new_scores = jnp.where(causal[None, :, None, None, :], new_scores, -jnp.inf)
    row_max = jnp.maximum(lax.optimization_barrier(jnp.max(old_scores, axis=-1)), lax.optimization_barrier(jnp.max(new_scores, axis=-1)))[..., None]
    old_exp = jnp.exp(old_scores - row_max)
    new_exp = jnp.exp(new_scores - row_max)
    exp_total = lax.optimization_barrier(jnp.sum(old_exp, axis=-1, keepdims=True)) + lax.optimization_barrier(jnp.sum(new_exp, axis=-1, keepdims=True))
    old_weights = (old_exp / exp_total).astype(jnp.bfloat16)
    new_weights = (new_exp / exp_total).astype(jnp.bfloat16)
    mixed_out = jnp.einsum('bskgc,bkcd->bskgd', old_weights.astype(jnp.float32), value_cache.astype(jnp.float32))
    mixed_out = mixed_out + jnp.einsum('bskgt,btkd->bskgd', new_weights.astype(jnp.float32), new_values.astype(jnp.float32))
    return mixed_out.astype(jnp.float32).reshape(seq_count, step_count, kv_heads * group_size * head_width)

def apply_adamw(master, moment_one, moment_two, gradient):
    first_new = beta_one * moment_one + (1.0 - beta_one) * gradient
    second_new = beta_two * moment_two + (1.0 - beta_two) * gradient * gradient
    first_hat = first_new / (1.0 - beta_one ** adam_step)
    second_hat = second_new / (1.0 - beta_two ** adam_step)
    updated = master - learn_rate * (first_hat / (jnp.sqrt(second_hat) + adam_eps) + decay_rate * master)
    return (updated, first_new, second_new)

def reference(layer_inputs, cotangent, master, moment_one, moment_two, embedding_table, token_ids, lengths, key_cache, value_cache):
    input_blocks = layer_inputs.reshape(N_DP, TOK_DEV, D)
    cot_blocks = cotangent.reshape(N_DP, TOK_DEV, QKV)

    def accumulate(running, block_pair):
        partial_grad = jnp.dot(block_pair[0].T, block_pair[1], preferred_element_type=jnp.float32).astype(jnp.bfloat16)
        return (running + lax.optimization_barrier(partial_grad).astype(jnp.float32), None)
    gradient, unused = lax.scan(accumulate, jnp.zeros((D, QKV), jnp.float32), (input_blocks, cot_blocks))
    new_master, new_moment_one, new_moment_two = apply_adamw(master, moment_one, moment_two, gradient)
    fresh = new_master.astype(jnp.bfloat16)
    embedded = embedding_table[token_ids]
    widened = embedded.astype(jnp.float32)
    normed = (widened * lax.rsqrt(lax.optimization_barrier(jnp.mean(widened * widened, axis=-1, keepdims=True)) + norm_eps)).astype(jnp.bfloat16)
    joined = jnp.dot(normed.reshape(SEQS * STEPS, D), fresh, preferred_element_type=jnp.float32)
    joined = joined.reshape(N_DP, SEQ_GRP, STEPS, QKV)

    def per_group(operands):
        return attend(operands[0], operands[1], operands[2], operands[3], QH // KVH)
    attended = lax.map(per_group, (joined, lengths.reshape(N_DP, SEQ_GRP), key_cache.reshape(N_DP, SEQ_GRP, KVH, CACHE, HD), value_cache.reshape(N_DP, SEQ_GRP, KVH, CACHE, HD)))
    attended = attended.reshape(SEQS, STEPS, QH * HD)
    return (new_master, new_moment_one, new_moment_two, attended)
```

```python
import math

import jax
import jax.numpy as jnp
from jax import lax
from jax.experimental import pallas as pl
from jax.experimental.pallas import tpu as pltpu
from jax.sharding import PartitionSpec as P

QH = 40
KVH = 8


beta_one = 0.9
beta_two = 0.95
adam_eps = 1e-08
learn_rate = 0.001
decay_rate = 0.1
adam_step = 8
norm_eps = 1e-06
rope_base = 1000000.0


def rotate(vectors, positions):
    half_width = vectors.shape[-1] // 2
    frequency = jnp.exp(
        jnp.arange(half_width, dtype=jnp.float32) * (-2.0 * math.log(rope_base) / vectors.shape[-1])
    )
    angles = positions[:, :, None, None, None].astype(jnp.float32) * frequency
    cosine_table = jnp.cos(angles)
    sine_table = jnp.sin(angles)
    front_half = vectors[..., :half_width]
    back_half = vectors[..., half_width:]
    return jnp.concatenate(
        [
            front_half * cosine_table - back_half * sine_table,
            back_half * cosine_table + front_half * sine_table,
        ],
        axis=-1,
    )


def attend(joined, lengths, key_cache, value_cache, group_size):
    seq_count = joined.shape[0]
    step_count = joined.shape[1]
    kv_heads = key_cache.shape[1]
    cache_span = key_cache.shape[2]
    head_width = key_cache.shape[3]
    shaped = joined.reshape(seq_count, step_count, kv_heads, group_size + 2, head_width)
    positions = lengths[:, None] + jnp.arange(step_count, dtype=jnp.int32)[None, :]
    queries = rotate(shaped[:, :, :, :group_size], positions)
    new_keys = rotate(shaped[:, :, :, group_size : group_size + 1], positions)[:, :, :, 0].astype(
        jnp.bfloat16
    )
    new_values = shaped[:, :, :, group_size + 1].astype(jnp.bfloat16)
    score_scale = 1.0 / math.sqrt(head_width)
    old_scores = (
        jnp.einsum(
            "bskgd,bkcd->bskgc",
            queries,
            key_cache.astype(jnp.float32),
            precision=lax.Precision.HIGHEST,
        )
        * score_scale
    )
    new_scores = (
        jnp.einsum(
            "bskgd,btkd->bskgt",
            queries,
            new_keys.astype(jnp.float32),
            precision=lax.Precision.HIGHEST,
        )
        * score_scale
    )
    cache_live = jnp.arange(cache_span, dtype=jnp.int32)[None, :] < lengths[:, None]
    old_scores = jnp.where(cache_live[:, None, None, None, :], old_scores, -jnp.inf)
    causal = jnp.arange(step_count)[None, :] <= jnp.arange(step_count)[:, None]
    new_scores = jnp.where(causal[None, :, None, None, :], new_scores, -jnp.inf)
    row_max = jnp.maximum(jnp.max(old_scores, axis=-1), jnp.max(new_scores, axis=-1))[..., None]
    old_exp = jnp.exp(old_scores - row_max)
    new_exp = jnp.exp(new_scores - row_max)
    exp_total = jnp.sum(old_exp, axis=-1, keepdims=True) + jnp.sum(new_exp, axis=-1, keepdims=True)
    old_weights = (old_exp / exp_total).astype(jnp.bfloat16)
    new_weights = (new_exp / exp_total).astype(jnp.bfloat16)
    mixed_out = jnp.einsum(
        "bskgc,bkcd->bskgd", old_weights, value_cache, preferred_element_type=jnp.float32
    )
    mixed_out = mixed_out + jnp.einsum(
        "bskgt,btkd->bskgd", new_weights, new_values, preferred_element_type=jnp.float32
    )
    return mixed_out.reshape(seq_count, step_count, kv_heads * group_size * head_width)


def apply_adamw(master, moment_one, moment_two, gradient):
    first_new = beta_one * moment_one + (1.0 - beta_one) * gradient
    second_new = beta_two * moment_two + (1.0 - beta_two) * gradient * gradient
    first_hat = first_new / (1.0 - beta_one**adam_step)
    second_hat = second_new / (1.0 - beta_two**adam_step)
    updated = master - learn_rate * (
        first_hat / (jnp.sqrt(second_hat) + adam_eps) + decay_rate * master
    )
    return (updated, first_new, second_new)


MESH = pl.DeviceIdType.MESH
CHUNKS = ((0, 0, 896), (1, 0, 512), (1, 512, 384))
ROUNDS = 5
R = 64


def place():
    d = lax.axis_index("dp")
    m = lax.axis_index("mp")
    return d // 4, (d // 2) % 2, d % 2, m // 2, m % 2


def at(z, h, c, x, l):
    return {"dp": z * 4 + h * 2 + c, "mp": x * 2 + l}


def remote(src, dst, send_sem, recv_sem, device):
    return pltpu.make_async_remote_copy(
        src_ref=src, dst_ref=dst, send_sem=send_sem, recv_sem=recv_sem,
        device_id=device, device_id_type=MESH,
    )


def gradient_kernel(
    x_ref, c_ref, g_ref,
    xt, xg, cg, sums0, sums1, sums2, part0, part1, part2,
    half_l0, half_l1, half_l2, half_r0, half_r1, half_r2,
    full_l0, full_l1, full_l2, full_r0, full_r1, full_r2,
    ysend0, ysend1, ysend2, one0, one1, one2, two1, two2,
    local_sem, swap_s, swap_r, own_s, own_r, fwd_s, fwd_r, csib_s, csib_r, cy_s, cy_r, cf_s, cf_r,
    hs, hr, fs, fr, ys, yr,
):
    z, h, c, x, l = place()
    sib = at(z, h, 1 - c, x, l)
    xr = at(z, h, c, (x + 1) % 4, l)
    xl = at(z, h, c, (x + 3) % 4, l)
    zr = at((z + 1) % 4, h, c, x, l)
    zl = at((z + 3) % 4, h, c, x, l)
    y_l = at(z, h, c, x, 1 - l)
    y_h = at(z, 1 - h, c, x, l)
    y_b = at(z, 1 - h, c, x, 1 - l)
    home = h == l
    sums = (sums0, sums1, sums2)
    part = (part0, part1, part2)
    half_l = (half_l0, half_l1, half_l2)
    half_r = (half_r0, half_r1, half_r2)
    full_l = (full_l0, full_l1, full_l2)
    full_r = (full_r0, full_r1, full_r2)
    ysend = (ysend0, ysend1, ysend2)
    one = (one0, one1, one2)
    two = (None, two1, two2)

    c_local = pltpu.make_async_copy(c_ref, cg.at[0, pl.ds(0, 1280)], local_sem)
    c_local.start()
    peers = (sib, xr, xl, zr, zl, y_l, y_h, y_b)
    barrier = pltpu.get_barrier_semaphore()
    for peer in peers:
        pl.semaphore_signal(barrier, inc=1, device_id=peer, device_id_type=MESH)
    pl.semaphore_wait(barrier, len(peers))

    started = []

    def go(copy):
        copy.start()
        started.append(copy)

    def c_cols(j):
        _, lo, width = CHUNKS[j]
        return pl.ds(lo, width)

    for j in (1, 2):
        go(remote(c_ref.at[:, c_cols(j)], cg.at[1, pl.ds(0, 1280), c_cols(j)], cy_s.at[j - 1], cy_r.at[j - 1], y_l))

    def transpose(j):
        block = x_ref[:, 128 * j : 128 * j + 128].T
        for s in range(2):
            feature = 128 * j + 64 * s
            xt[feature // 320, feature % 320 : feature % 320 + 64, :] = block[64 * s : 64 * s + 64]

    def rows(k):
        return pl.ds(R * k, R)

    def swap(k):
        go(remote(xt.at[1 - c, rows(k)], xg.at[x, rows(k), pl.ds(1280, 1280)], swap_s.at[k], swap_r.at[k], sib))
        xg[x, R * k : R * k + R, 0:1280] = xt[c, R * k : R * k + R, :]

    transpose(0)
    transpose(2)
    swap(0)
    go(remote(c_ref, cg.at[0, pl.ds(1280, 1280)], csib_s, csib_r, sib))
    transpose(3)
    swap(1)
    transpose(1)
    swap(2)
    transpose(4)
    swap(3)
    swap(4)

    x_left, x_right, x_far = (x + 3) % 4, (x + 1) % 4, (x + 2) % 4

    def send_own(k):
        landed = xg.at[x, rows(k), pl.ds(1280, 1280)]
        remote(landed, landed, swap_s.at[k], swap_r.at[k], sib).wait_recv()
        block = xg.at[x, rows(k)]
        go(remote(block, block, own_s.at[0, k], own_r.at[0, k], xr))
        go(remote(block, block, own_s.at[1, k], own_r.at[1, k], xl))

    def far_rows(k, side):
        return pl.ds(R * k + side * (R // 2), R // 2)

    def forward(k):
        block = xg.at[x_left, rows(k)]
        remote(block, block, own_s.at[0, k], own_r.at[0, k], xr).wait_recv()
        block = xg.at[x_left, far_rows(k, 0)]
        go(remote(block, block, fwd_s.at[0, k], fwd_r.at[0, k], xr))
        block = xg.at[x_right, rows(k)]
        remote(block, block, own_s.at[1, k], own_r.at[1, k], xl).wait_recv()
        block = xg.at[x_right, far_rows(k, 1)]
        go(remote(block, block, fwd_s.at[1, k], fwd_r.at[1, k], xl))

    def wait_far(k):
        for side, device in ((0, xr), (1, xl)):
            block = xg.at[x_far, far_rows(k, side)]
            remote(block, block, fwd_s.at[side, k], fwd_r.at[side, k], device).wait_recv()

    def c_forward(j):
        block = cg.at[1, pl.ds(0, 1280), c_cols(j)]
        remote(block, block, cy_s.at[j - 1], cy_r.at[j - 1], y_l).wait_recv()
        go(remote(block, cg.at[1, pl.ds(1280, 1280), c_cols(j)], cf_s.at[j - 1], cf_r.at[j - 1], sib))

    def c_wait(j):
        block = cg.at[1, pl.ds(1280, 1280), c_cols(j)]
        remote(block, block, cf_s.at[j - 1], cf_r.at[j - 1], sib).wait_recv()

    low, high = slice(0, R // 2), slice(R // 2, R)
    dlow, dhigh = pl.ds(0, R // 2), pl.ds(R // 2, R // 2)

    def multiply(k, j):
        half, lo, width = CHUNKS[j]
        lhs = jnp.concatenate([xg[(z + r) % 4, R * k : R * k + R, :] for r in range(4)], axis=0)
        product = jnp.dot(lhs, cg[half, :, lo : lo + width], preferred_element_type=jnp.float32)
        sums[j][k] = product[0:R]
        for r in (1, 2, 3):
            part[j][r - 1, k] = product[R * r : R * r + R].astype(jnp.bfloat16)
        go(remote(part[j].at[1, k, dlow], half_l[j].at[k], hs.at[0, j, k], hr.at[0, j, k], zr))
        go(remote(part[j].at[1, k, dhigh], half_r[j].at[k], hs.at[1, j, k], hr.at[1, j, k], zl))

    def combine(k, j):
        remote(half_l[j].at[k], half_l[j].at[k], hs.at[0, j, k], hr.at[0, j, k], zr).wait_recv()
        part[j][0, k, low] = (part[j][0, k, low].astype(jnp.float32) + half_l[j][k].astype(jnp.float32)).astype(jnp.bfloat16)
        go(remote(part[j].at[0, k], full_l[j].at[k], fs.at[0, j, k], fr.at[0, j, k], zr))
        remote(half_r[j].at[k], half_r[j].at[k], hs.at[1, j, k], hr.at[1, j, k], zl).wait_recv()
        part[j][2, k, high] = (part[j][2, k, high].astype(jnp.float32) + half_r[j][k].astype(jnp.float32)).astype(jnp.bfloat16)
        go(remote(part[j].at[2, k], full_r[j].at[k], fs.at[1, j, k], fr.at[1, j, k], zl))

    def y_copies(k, j):
        src = ysend[j].at[k]
        if j == 0:
            return None, remote(src, one[j].at[k], ys.at[j, k], yr.at[0, j, k], y_h)
        return (
            remote(src, one[j].at[k], ys.at[j, k], yr.at[0, j, k], y_l),
            remote(src, two[j].at[k], ys.at[j, k], yr.at[1, j, k], y_b),
        )

    def total(k, j):
        remote(full_l[j].at[k], full_l[j].at[k], fs.at[0, j, k], fr.at[0, j, k], zr).wait_recv()
        remote(full_r[j].at[k], full_r[j].at[k], fs.at[1, j, k], fr.at[1, j, k], zl).wait_recv()
        value = sums[j][k] + full_l[j][k].astype(jnp.float32) + full_r[j][k].astype(jnp.float32)
        at_home, away = y_copies(k, j)
        if j == 0:
            sums[j][k] = value
        ysend[j][k] = value.astype(jnp.bfloat16)
        if at_home is not None:
            pl.when(home)(at_home.start)
        pl.when(jnp.logical_not(home))(away.start)

    def finish(k, j):
        at_home, away = y_copies(k, j)
        _, lo, width = CHUNKS[j]
        if j == 0:
            @pl.when(home)
            def _():
                away.wait_recv()
                g_ref[R * k : R * k + R, :] = sums[j][k] + one[j][k].astype(jnp.float32)
        else:
            @pl.when(jnp.logical_not(home))
            def _():
                at_home.wait_recv()
                away.wait_recv()
                g_ref[R * k : R * k + R, lo : lo + width] = one[j][k].astype(jnp.float32) + two[j][k].astype(jnp.float32)

    order = []

    def step(tile):
        order.append(tile)
        n = len(order)
        if tile is not None:
            multiply(*tile)
        for lag, stage in ((1, combine), (2, total), (3, finish)):
            if n > lag and order[n - 1 - lag] is not None:
                stage(*order[n - 1 - lag])

    send_own(0)
    send_own(1)
    landed = cg.at[0, pl.ds(1280, 1280)]
    forward(0)
    send_own(2)
    c_local.wait()
    remote(landed, landed, csib_s, csib_r, sib).wait_recv()
    forward(1)
    send_own(3)
    wait_far(0)
    step((0, 0))
    forward(2)
    send_own(4)
    wait_far(1)
    step((1, 0))
    c_forward(1)
    forward(3)
    wait_far(2)
    step((2, 0))
    c_wait(1)
    step((0, 1))
    step((1, 1))
    step((2, 1))
    forward(4)
    wait_far(3)
    step((3, 0))
    step((3, 1))
    c_forward(2)
    wait_far(4)
    step((4, 0))
    step((4, 1))
    c_wait(2)
    for k in range(5):
        step((k, 2))
    for _ in range(3):
        step(None)

    for copy in started:
        copy.wait_send()
    for j in range(3):
        for k in range(5):
            at_home, away = y_copies(k, j)
            if at_home is not None:
                pl.when(home)(at_home.wait_send)
            pl.when(jnp.logical_not(home))(away.wait_send)


def gradient_of(layer_inputs, cotangent):
    bf, f32 = jnp.bfloat16, jnp.float32
    widths = [width for _, _, width in CHUNKS]
    dma = pltpu.SemaphoreType.DMA
    vm = pltpu.VMEM
    scratch = [vm((2, 320, 1280), bf), vm((4, 320, 2560), bf), vm((2, 2560, 896), bf)]
    scratch += [vm((5, R, w), f32) for w in widths]
    scratch += [vm((3, 5, R, w), bf) for w in widths]
    scratch += [vm((5, R // 2, w), bf) for w in widths] * 2
    scratch += [vm((5, R, w), bf) for w in widths] * 2
    scratch += [vm((5, R, w), bf) for w in widths]
    scratch += [vm((5, R, w), bf) for w in widths]
    scratch += [vm((5, R, w), bf) for w in widths[1:]]
    scratch += [
        dma(()), dma((5,)), dma((5,)), dma((2, 5)), dma((2, 5)), dma((2, 5)), dma((2, 5)),
        dma(()), dma(()), dma((2,)), dma((2,)), dma((2,)), dma((2,)),
        dma((2, 3, 5)), dma((2, 3, 5)), dma((2, 3, 5)), dma((2, 3, 5)), dma((3, 5)), dma((2, 3, 5)),
    ]
    return pl.pallas_call(
        gradient_kernel,
        out_shape=jax.ShapeDtypeStruct((320, 896), f32),
        in_specs=[pl.BlockSpec(memory_space=pltpu.VMEM), pl.BlockSpec(memory_space=pl.ANY)],
        out_specs=pl.BlockSpec(memory_space=pltpu.VMEM),
        scratch_shapes=scratch,
        compiler_params=pltpu.CompilerParams(
            collective_id=1, has_side_effects=True, vmem_limit_bytes=60 * 1024 * 1024
        ),
        cost_estimate=pl.CostEstimate(flops=11_700_000_000, bytes_accessed=5_000_000, transcendentals=0),
        name="gradient",
    )(layer_inputs, cotangent)


def local(
    layer_inputs,
    cotangent,
    master,
    moment_one,
    moment_two,
    embedding_table,
    token_ids,
    lengths,
    key_cache,
    value_cache,
):
    gradient = gradient_of(layer_inputs, cotangent)
    new_master, new_moment_one, new_moment_two = apply_adamw(
        master, moment_one, moment_two, gradient
    )
    fresh = new_master.astype(jnp.bfloat16)
    vocab_rows = embedding_table.shape[0]
    offset = lax.axis_index("dp") * vocab_rows
    shifted = token_ids - offset
    inside = (shifted >= 0) & (shifted < vocab_rows)
    picked = jnp.take(embedding_table, jnp.clip(shifted, 0, vocab_rows - 1), axis=0)
    picked = jnp.where(inside[:, :, None], picked.astype(jnp.float32), 0.0)
    own_rows = lax.psum_scatter(picked.astype(jnp.bfloat16), "dp", scatter_dimension=0, tiled=True)
    embedded = lax.all_gather(own_rows, "mp", axis=2, tiled=True)
    widened = embedded.astype(jnp.float32)
    normed = (
        widened * lax.rsqrt(jnp.mean(widened * widened, axis=-1, keepdims=True) + norm_eps)
    ).astype(jnp.bfloat16)
    seq_count = normed.shape[0]
    step_count = normed.shape[1]
    model_width = normed.shape[2]
    flat_rows = normed.reshape(seq_count * step_count, model_width)
    joined = jnp.dot(
        flat_rows,
        lax.all_gather(fresh, "dp", axis=0, tiled=True),
        preferred_element_type=jnp.float32,
    )
    joined = joined.reshape(seq_count, step_count, fresh.shape[1])
    attended = attend(joined, lengths, key_cache, value_cache, QH // KVH)
    return (new_master, new_moment_one, new_moment_two, attended)


def solution(mesh):
    in_specs = (
        P("dp", "mp"),
        P("dp", "mp"),
        P("dp", "mp"),
        P("dp", "mp"),
        P("dp", "mp"),
        P("dp", "mp"),
        P(),
        P("dp"),
        P("dp", "mp", None, None),
        P("dp", "mp", None, None),
    )
    out_specs = (P("dp", "mp"), P("dp", "mp"), P("dp", "mp"), P("dp", None, "mp"))
    return jax.shard_map(local, mesh=mesh, in_specs=in_specs, out_specs=out_specs, check_vma=False)
```
